32 devices in a mesh: run: 4 (over z), feat: 2 (over core), vox: 4 (over y, x).
Axes of the slice: x: 2, y: 2, z: 4, core: 2. Of those that a mesh axis runs over, the one named last changes fastest.
Arguments:
- stimulus: bfloat16 [4, 512, 256], P('run', None, 'feat')
- responses: bfloat16 [4, 512, 512], P('run', None, 'vox')
- run_lengths: int32 [4], P('run'), may hold values from 1 to 512, 1536 in all
- lag_steps: int32 [4], replicated, may hold values from 0 to 7, as said below
- ridge_grid: float32 [16], replicated, may hold values from 0.05 to 5
- ridge_pick: int32 [4, 2], P('run'), may hold values from 0 to 15
Outputs:
- weights: float32 [4, 2, 1024, 512], P('run', None, 'feat', 'vox')
- fold_errors: float32 [4, 2, 512], P('run', None, 'vox')
The draws below stay inside these ranges and needn't reach their ends.
Inputs may be any that keep to these rules, and one draw needn't show every extreme that they name: lag_steps[j] is 2 j or 2 j + 1; lag_steps[0] is 0 and the last entry is 7.
All inputs are finite; a program needn't handle non-finite values. No bound on the sum of `run_lengths` on one device may be relied on, other than what follows from the above.
Results may differ from the reference program's by a relative error of at most 0.0003.
Values may be sent and summed in bfloat16 or wider, within the bound.
A program may use at most 128 MiB of HBM per device.

```python
import math
import jax
import jax.numpy as jnp
import numpy as np
from jax import lax

E = 256
NLAG = 4
NP = 2
NPEN = 16
TRM = 512
F = 1024
RUNS = 4
VOX = 512


def stimulus_field(key):
    base = jax.random.fold_in(key, 101)
    noise = jax.random.normal(jax.random.fold_in(base, 1), (RUNS, TRM + 1, E), jnp.float32)
    current = noise[:, 1:, :]
    earlier = noise[:, :-1, :]
    return current + 0.7 * earlier + 0.5 * jnp.roll(current, 1, axis=2)


def draw_stimulus(key, part):
    return stimulus_field(key).astype(jnp.bfloat16)


def draw_responses(key, part):
    field = stimulus_field(key)
    column = jnp.arange(VOX, dtype=jnp.int32) % E
    picked = field[:, :, column]
    amplitude = 0.3 + 1.2 * jax.random.uniform(jax.random.fold_in(key, 201), (RUNS,), jnp.float32)
    voxel_gain = 0.5 + jax.random.uniform(jax.random.fold_in(key, 202), (VOX,), jnp.float32)
    noise = jax.random.normal(jax.random.fold_in(key, 203), (RUNS, TRM, VOX), jnp.float32)
    values = amplitude[:, None, None] * voxel_gain[None, None, :] * picked + 0.6 * noise
    return values.astype(jnp.bfloat16)


def draw_lag_steps(key, part):
    extra = jax.random.randint(jax.random.fold_in(key, 301), (NLAG,), 0, 2, jnp.int32)
    extra = extra.at[0].set(0)
    extra = extra.at[NLAG - 1].set(1)
    return jnp.arange(NLAG, dtype=jnp.int32) * 2 + extra


def place_ends(result, rng, low, top_value):
    extent = result.shape
    place = [jax.random.randint(jax.random.fold_in(rng, axis), (), 0, extent[axis]) for axis in range(len(extent))]
    result = result.at[tuple(place)].set(low)
    longest = extent.index(max(extent))
    place[longest] = (place[longest] + 1) % extent[longest]
    return result.at[tuple(place)].set(top_value)


def profile(number_of, total, most, lean):
    loads = [(1 << 20) // math.isqrt(standing ** lean) + 1 for standing in range(2, number_of + 1)]
    rest, given = total - most - (number_of - 1), [1] * (number_of - 1)
    while rest > 0:
        candidates = [i for i in range(number_of - 1) if given[i] < most]
        whole, budget = sum([loads[i] for i in candidates]), rest
        for i in candidates:
            more = min(most - given[i], max(1, budget * loads[i] // whole), rest)
            given[i] = given[i] + more
            rest = rest - more
    return np.array([most] + given)


def ragged(key, amount, total, bound, skew):
    if amount == 2:
        one = jax.random.randint(key, (), max(1, total - bound), min(bound, total - 1) + 1)
        return jnp.stack([one, total - one])
    sizes = jnp.asarray(profile(amount, total, bound, skew), jnp.int32)
    twos = (amount - 1) // 2
    giver, receiver = sizes[1:1 + 2 * twos:2], sizes[2:2 + 2 * twos:2]
    margin = jnp.minimum(giver - 1, bound - receiver)
    moved = jax.random.randint(jax.random.fold_in(key, 1), (twos,), 0, 1 << 20) % (margin + 1)
    sizes = sizes.at[1:1 + 2 * twos:2].set(giver - moved).at[2:2 + 2 * twos:2].set(receiver + moved)
    return sizes[jax.random.permutation(jax.random.fold_in(key, 2), amount)]


def setup_inputs(seed: int = 0) -> dict:
    key_of = jax.random.split(jax.random.key(seed), 7)
    return {
        "stimulus": draw_stimulus(jax.random.fold_in(key_of[6], 71), 0),
        "responses": draw_responses(jax.random.fold_in(key_of[6], 71), 0),
        "run_lengths": ragged(key_of[2], RUNS, RUNS * TRM * 3 // 4, TRM, 0).astype(jnp.int32),
        "lag_steps": draw_lag_steps(jax.random.fold_in(key_of[6], 71), 0),
        "ridge_grid": jnp.clip(jnp.exp(jax.random.uniform(key_of[4], (NPEN,), jnp.float32, math.log(0.05), math.log(5.0))), 0.05, 5.0),
        "ridge_pick": place_ends(jax.random.randint(key_of[5], (RUNS, NP), 0, NPEN), jax.random.fold_in(key_of[5], 1), 0, NPEN - 1).astype(jnp.int32),
    }


def build_features(stim_run, lag_steps, length):
    steps_t = jnp.arange(TRM, dtype=jnp.int32)
    pieces = []
    for j in range(NLAG):
        lag = lag_steps[j]
        shifted = jnp.roll(stim_run, lag, axis=0)
        keep = (steps_t >= lag) & (steps_t < length)
        pieces.append(jnp.where(keep[:, None], shifted, jnp.zeros_like(shifted)))
    stacked = jnp.stack(pieces, axis=2)
    return stacked.reshape(TRM, E * NLAG)

def run_terms(stimulus, responses, run_lengths, lag_steps, index):
    length = run_lengths[index]
    feats = build_features(stimulus[index], lag_steps, length)
    steps_t = jnp.arange(TRM, dtype=jnp.int32)
    masked = jnp.where((steps_t < length)[:, None], responses[index], jnp.zeros_like(responses[index]))
    gram = jnp.dot(feats.T.astype(jnp.float32), feats.astype(jnp.float32), preferred_element_type=jnp.float32)
    cross = jnp.dot(feats.T.astype(jnp.float32), masked.astype(jnp.float32), preferred_element_type=jnp.float32)
    return (feats, masked, gram, cross)

def solve_fold(gram_s, cross_s, penalty, feats, masked, length):
    width = gram_s.shape[0]
    eye = jnp.eye(width, dtype=jnp.float32)
    system = gram_s[None] + penalty[:, None, None] * eye[None]
    lower = jnp.linalg.cholesky(system)
    rhs = jnp.broadcast_to(cross_s[None], (penalty.shape[0],) + cross_s.shape)
    inner = lax.linalg.triangular_solve(lower, rhs, left_side=True, lower=True, transpose_a=False)
    weights = lax.linalg.triangular_solve(lower, inner, left_side=True, lower=True, transpose_a=True)
    predicted = jnp.einsum('tf,pfv->ptv', feats.astype(jnp.float32), weights, precision=lax.Precision.HIGHEST)
    errors = jnp.sum((masked.astype(jnp.float32)[None] - predicted) ** 2, axis=1) / length.astype(jnp.float32)
    return (weights, errors)

def reference(stimulus, responses, run_lengths, lag_steps, ridge_grid, ridge_pick):

    def accumulate(carry, index):
        feats, masked, gram, cross = run_terms(stimulus, responses, run_lengths, lag_steps, index)
        return ((carry[0] + gram, carry[1] + cross), None)
    start = (jnp.zeros((F, F), jnp.float32), jnp.zeros((F, VOX), jnp.float32))
    totals, unused = lax.scan(accumulate, start, jnp.arange(RUNS, dtype=jnp.int32))
    count_all = jnp.sum(run_lengths).astype(jnp.float32)

    def fold(index):
        feats, masked, gram, cross = run_terms(stimulus, responses, run_lengths, lag_steps, index)
        length = run_lengths[index]
        rest_count = count_all - length.astype(jnp.float32)
        rest_gram = (totals[0] - gram) / rest_count
        rest_cross = (totals[1] - cross) / rest_count
        penalty = ridge_grid[ridge_pick[index]]
        return solve_fold(rest_gram, rest_cross, penalty, feats, masked, length)
    weights, fold_errors = lax.map(fold, jnp.arange(RUNS, dtype=jnp.int32))
    return (weights, fold_errors)
```

```python
import functools

import jax
import jax.numpy as jnp
from jax import lax
from jax.experimental import pallas as pl
from jax.experimental.pallas import tpu as pltpu
from jax.sharding import PartitionSpec as P

MESH = pl.DeviceIdType.MESH
B = 128
SUB = 8
F32 = jnp.float32
BF16 = jnp.bfloat16
HI = lax.Precision.HIGHEST


def gather_kernel(runs, stim, resp, length, stim_all, resp_all, len_all, own_sem, s1, r1, s2, r2):
    me = lax.axis_index("run")
    core = lax.axis_index("feat")
    other = 1 - core
    half = resp.shape[0] // 2
    rows = pl.ds(pl.multiple_of(core * half, 16), half)
    barrier = pltpu.get_barrier_semaphore()
    for d in range(1, runs):
        pl.semaphore_signal(
            barrier, inc=1, device_id={"run": lax.rem(me + d, runs)}, device_id_type=MESH
        )
    pl.semaphore_signal(barrier, inc=1, device_id={"feat": other}, device_id_type=MESH)
    pl.semaphore_wait(barrier, runs)

    def to_run(src, dst, which, d):
        return pltpu.make_async_remote_copy(
            src_ref=src,
            dst_ref=dst,
            send_sem=s1.at[which, d - 1],
            recv_sem=r1.at[which, d - 1],
            device_id={"run": lax.rem(me + d, runs)},
            device_id_type=MESH,
        )

    def to_core(src, which, d):
        return pltpu.make_async_remote_copy(
            src_ref=src,
            dst_ref=src,
            send_sem=s2.at[which, d],
            recv_sem=r2.at[which, d],
            device_id={"feat": other},
            device_id_type=MESH,
        )

    first = []
    for d in range(1, runs):
        first.append(
            (
                to_run(stim, stim_all.at[d, core], 0, d),
                to_run(resp.at[rows], resp_all.at[d - 1, rows], 1, d),
                to_run(length, len_all.at[d - 1], 2, d),
            )
        )
    for trio in first:
        for copy in trio:
            copy.start()
    own = pltpu.make_async_copy(stim, stim_all.at[0, core], own_sem)
    own.start()
    own.wait()
    second = [to_core(stim_all.at[0, core], 0, 0)]
    second[0].start()
    for d in range(1, runs):
        first[d - 1][0].wait_recv()
        a = to_core(stim_all.at[d, core], 0, d)
        a.start()
        first[d - 1][1].wait_recv()
        b = to_core(resp_all.at[d - 1, rows], 1, d)
        b.start()
        first[d - 1][2].wait_recv()
        second += [a, b]
    for trio in first:
        for copy in trio:
            copy.wait_send()
    for copy in second:
        copy.wait()


def gather(stim, resp, length, runs):
    time, width = stim.shape
    vox = resp.shape[1]
    anyspace = pl.BlockSpec(memory_space=pl.ANY)
    return pl.pallas_call(
        functools.partial(gather_kernel, runs),
        out_shape=(
            jax.ShapeDtypeStruct((runs, 2, time, width), stim.dtype),
            jax.ShapeDtypeStruct((runs - 1, time, vox), resp.dtype),
            jax.ShapeDtypeStruct((runs - 1, 8, 128), jnp.int32),
        ),
        in_specs=[anyspace] * 3,
        out_specs=(anyspace,) * 3,
        scratch_shapes=[
            pltpu.SemaphoreType.DMA,
            pltpu.SemaphoreType.DMA((3, runs - 1)),
            pltpu.SemaphoreType.DMA((3, runs - 1)),
            pltpu.SemaphoreType.DMA((2, runs)),
            pltpu.SemaphoreType.DMA((2, runs)),
        ],
        compiler_params=pltpu.CompilerParams(collective_id=0, has_side_effects=True),
    )(stim, resp, length)


def invert(block):
    count = B // SUB
    rows = [block[SUB * i : SUB * (i + 1), :] for i in range(count)]
    lane = lax.broadcasted_iota(jnp.int32, (SUB, B), 1)
    sub = lax.broadcasted_iota(jnp.int32, (SUB, B), 0)

    def wide(x):
        return jnp.broadcast_to(x, (SUB, B))

    for s in range(count):
        at = SUB * s
        inside = (lane >= at) & (lane < at + SUB)
        panel = rows[s]
        cols = [wide(panel[:, at + j : at + j + 1]) for j in range(SUB)]
        e = [[wide(cols[j][i : i + 1, :]) for j in range(i + 1)] for i in range(SUB)]
        start = jnp.where(inside, jnp.where(lane == at + sub, 1.0, 0.0), panel)
        r = [wide(start[i : i + 1, :]) for i in range(SUB)]
        scale, low = [], []
        for p in range(SUB):
            q = 1.0 / e[p][p]
            scale.append(q)
            l = {i: e[i][p] * q for i in range(p + 1, SUB)}
            low.append(l)
            for i in range(p + 1, SUB):
                for j in range(p + 1, i + 1):
                    e[i][j] = e[i][j] - l[i] * e[j][p]
            for i in range(p + 1, SUB):
                r[i] = r[i] - l[i] * r[p]
        for p in range(SUB):
            r[p] = r[p] * scale[p]
        for i in range(SUB - 1, 0, -1):
            for p in range(i):
                r[p] = r[p] - low[p][i] * r[i]
        order = [(s + 1 + t) % count for t in range(count - 1)]
        for t in order:
            row = rows[t]
            acc = jnp.where(inside, 0.0, row)
            for p in range(SUB):
                acc = acc - wide(row[:, at + p : at + p + 1]) * r[p]
            rows[t] = acc
        new = r[0]
        for i in range(1, SUB):
            new = jnp.where(sub == i, r[i], new)
        rows[s] = new
    return jnp.concatenate(rows, axis=0)


def solve_kernel(
    lags, grid, pick, stim, resp, lens, own_resp, own_len, w_out, err_out, xs, phi, tgt, m, pinv
):
    others, time, vox = resp.shape
    nlag = lags.shape[0]
    feat = stim.shape[1]
    width = feat * nlag * B
    blocks = width // B
    chunk = others if others <= 4 else 1
    steps = lax.broadcasted_iota(jnp.int32, (time, B), 0)

    def features(run, length, at):
        keep = steps < length
        for f in range(feat):
            xs[pl.ds(8, time), :] = stim[run, f].astype(F32)
            for j in range(nlag):
                moved = xs[pl.ds(8 - lags[j], time), :]
                phi[pl.ds(at, time), pl.ds((f * nlag + j) * B, B)] = jnp.where(
                    keep, moved, 0.0
                ).astype(BF16)

    def products(total, first):
        full = total.shape[0]
        for i in range(0, blocks, 2):
            lhs = total[:, i * B : (i + 2) * B]
            part = lax.dot_general(
                lhs, total[:, i * B :], (((0,), (0,)), ((), ())), preferred_element_type=F32
            )
            if first:
                m[i * B : (i + 2) * B, i * B : width] = part
            else:
                m[i * B : (i + 2) * B, i * B : width] += part
        part = lax.dot_general(
            total, tgt[:full, :], (((0,), (0,)), ((), ())), preferred_element_type=F32
        )
        if first:
            m[:, width:] = part
        else:
            m[:, width:] += part

    xs[pl.ds(0, 8), :] = jnp.zeros((8, B), F32)
    if chunk == others:
        for i in range(others):
            features(i + 1, lens[i, 0:1, :], i * time)
            tgt[pl.ds(i * time, time), :] = resp[i]
        products(phi[...], True)
    else:
        m[...] = jnp.zeros_like(m)

        def one(i, c):
            features(i + 1, lens[i, 0:1, :], 0)
            tgt[...] = resp[i]
            products(phi[...], False)
            return c

        lax.fori_loop(0, others, one, 0)

    count = jnp.sum(lens[:, 0, :], axis=0, keepdims=True).astype(F32)
    ridge = grid[pick[0, lax.axis_index("feat")]] * count
    diag = lax.broadcasted_iota(jnp.int32, (B, B), 0) == lax.broadcasted_iota(
        jnp.int32, (B, B), 1
    )
    shift = jnp.where(diag, ridge, 0.0)

    def step(k, c):
        base = pl.multiple_of(k * B, B)
        pinv[...] = invert(m[pl.ds(base, B), pl.ds(base, B)] + shift)
        for kk in range(blocks):

            @pl.when(k == kk)
            def _():
                lo = (kk + 1) * B
                u = m[kk * B : lo, lo:]
                v = jnp.dot(pinv[...], u, precision=HI, preferred_element_type=F32)
                for i in range(kk + 1, blocks, 2):
                    n = min(2, blocks - i)
                    off = i * B - lo
                    m[i * B : (i + n) * B, i * B :] -= lax.dot_general(
                        u[:, off : off + n * B],
                        v[:, off:],
                        (((0,), (0,)), ((), ())),
                        precision=HI,
                        preferred_element_type=F32,
                    )
                m[kk * B : lo, lo:] = v

        return c

    lax.fori_loop(0, blocks, step, 0)

    for k in range(blocks - 2, -1, -1):
        lo = (k + 1) * B
        m[k * B : lo, width:] -= jnp.dot(
            m[k * B : lo, lo:width], m[lo:, width:], precision=HI, preferred_element_type=F32
        )
    x = m[:, width:]
    for f in range(feat):
        for j in range(nlag):
            w_out[f, pl.ds(j, B, stride=nlag), :] = x[(f * nlag + j) * B : (f * nlag + j + 1) * B]
    top = x.astype(BF16)
    rest = x - top.astype(F32)
    mid = rest.astype(BF16)
    low = (rest - mid.astype(F32)).astype(BF16)
    features(0, own_len[0:1, :], 0)
    made = jnp.dot(
        phi[:time, :], jnp.concatenate([top, mid, low], axis=1), preferred_element_type=F32
    )
    made = made[:, :vox] + (made[:, vox : 2 * vox] + made[:, 2 * vox :])
    target = jnp.where(steps < own_len[0:1, :], own_resp[...].astype(F32), 0.0)
    error = jnp.sum((target - made) ** 2, axis=0, keepdims=True)
    err_out[...] = jnp.broadcast_to(error / own_len[0:1, :].astype(F32), err_out.shape)


def solve(lags, grid, pick, stim, resp, lens, own_resp, own_len):
    others, time, vox = resp.shape
    feat = stim.shape[1]
    width = feat * lags.shape[0] * B
    depth = time * (others if others <= 4 else 1)
    vmem = pl.BlockSpec(memory_space=pltpu.VMEM)
    smem = pl.BlockSpec(memory_space=pltpu.SMEM)
    return pl.pallas_call(
        solve_kernel,
        out_shape=(
            jax.ShapeDtypeStruct((feat, width // feat, vox), F32),
            jax.ShapeDtypeStruct((8, vox), F32),
        ),
        in_specs=[smem] * 3 + [vmem] * 5,
        out_specs=(vmem, vmem),
        scratch_shapes=[
            pltpu.VMEM((time + 8, B), F32),
            pltpu.VMEM((depth, width), BF16),
            pltpu.VMEM((depth, vox), BF16),
            pltpu.VMEM((width, width + vox), F32),
            pltpu.VMEM((B, B), F32),
        ],
        compiler_params=pltpu.CompilerParams(vmem_limit_bytes=56 * 1024 * 1024),
    )(lags, grid, pick, stim, resp, lens, own_resp, own_len)


def swap_kernel(w, err, w_all, err_all, send, recv, local):
    core = lax.axis_index("feat")
    other = 1 - core
    barrier = pltpu.get_barrier_semaphore()
    pl.semaphore_signal(barrier, inc=1, device_id={"feat": other}, device_id_type=MESH)
    pl.semaphore_wait(barrier, 1)
    copies = [
        pltpu.make_async_remote_copy(
            src_ref=src,
            dst_ref=dst,
            send_sem=send.at[i],
            recv_sem=recv.at[i],
            device_id={"feat": other},
            device_id_type=MESH,
        )
        for i, (src, dst) in enumerate(((w.at[other], w_all.at[core]), (err, err_all.at[core])))
    ]
    copies += [
        pltpu.make_async_copy(w.at[core], w_all.at[core], local.at[0]),
        pltpu.make_async_copy(err, err_all.at[core], local.at[1]),
    ]
    for copy in copies:
        copy.start()
    for copy in copies:
        copy.wait()


def swap(w, err):
    anyspace = pl.BlockSpec(memory_space=pl.ANY)
    return pl.pallas_call(
        swap_kernel,
        out_shape=(
            jax.ShapeDtypeStruct(w.shape, F32),
            jax.ShapeDtypeStruct((2,) + err.shape, F32),
        ),
        in_specs=[anyspace] * 2,
        out_specs=(anyspace,) * 2,
        scratch_shapes=[pltpu.SemaphoreType.DMA((2,))] * 3,
        compiler_params=pltpu.CompilerParams(collective_id=1, has_side_effects=True),
    )(w, err)


def local(stimulus, responses, run_lengths, lag_steps, ridge_grid, ridge_pick):
    runs = lax.axis_size("run")
    length = jnp.broadcast_to(run_lengths.reshape(1, 1), (8, 128))
    stim_all, resp_all, len_all = gather(stimulus[0], responses[0], length, runs)
    w, err = solve(
        lag_steps, ridge_grid, ridge_pick, stim_all, resp_all, len_all, responses[0], length
    )
    w_all, err_all = swap(w, err)
    return (w_all[None], err_all[:, 0, :][None])


def solution(mesh):
    return jax.shard_map(
        local,
        mesh=mesh,
        in_specs=(
            P("run", None, "feat"),
            P("run", None, "vox"),
            P("run"),
            P(),
            P(),
            P("run", None),
        ),
        out_specs=(P("run", None, "feat", "vox"), P("run", None, "vox")),
        check_vma=False,
    )
```

```python
import functools

import jax
import jax.numpy as jnp
from jax import lax
from jax.experimental import pallas as pl
from jax.experimental.pallas import tpu as pltpu
from jax.sharding import PartitionSpec as P

MESH = pl.DeviceIdType.MESH
B = 128
SUB = 8
F32 = jnp.float32
BF16 = jnp.bfloat16
HI = lax.Precision.HIGHEST


def gather_kernel(
    runs, parts, stim, resp, length, stim_all, resp_all, len_all, own_sem, s1, r1, s2, r2, s3, r3
):
    me = lax.axis_index("run")
    place = lax.axis_index("vox")
    core = lax.axis_index("feat")
    other = 1 - core
    half = resp.shape[0] // 2
    piece = stim.shape[0] // parts
    rows = pl.ds(pl.multiple_of(core * half, 16), half)
    mine = pl.ds(pl.multiple_of(place * piece, 16), piece)
    barrier = pltpu.get_barrier_semaphore()
    peers = [{"run": lax.rem(me + d, runs)} for d in range(1, runs)]
    peers += [{"vox": lax.rem(place + d, parts)} for d in range(1, parts)]
    peers += [{"feat": other}]
    for peer in peers:
        pl.semaphore_signal(barrier, inc=1, device_id=peer, device_id_type=MESH)
    own = pltpu.make_async_copy(stim, stim_all.at[0, core], own_sem)
    own.start()
    pl.semaphore_wait(barrier, len(peers))

    def remote(src, dst, send, recv, peer):
        return pltpu.make_async_remote_copy(
            src_ref=src,
            dst_ref=dst,
            send_sem=send,
            recv_sem=recv,
            device_id=peer,
            device_id_type=MESH,
        )

    def to_run(src, dst, which, d):
        peer = {"run": lax.rem(me + d, runs)}
        return remote(src, dst, s1.at[which, d - 1], r1.at[which, d - 1], peer)

    def to_core(src, dst, which, d):
        return remote(src, dst, s3.at[which, d], r3.at[which, d], {"feat": other})

    first = [None]
    for d in range(1, runs):
        first.append(
            (
                to_run(stim.at[mine], stim_all.at[d, core, mine], 0, d),
                to_run(resp.at[rows], resp_all.at[d - 1, rows], 1, d),
                to_run(length, len_all.at[d - 1], 2, d),
            )
        )
    for which in range(3):
        for d in range(1, runs):
            first[d][which].start()
    third = [to_core(stim, stim_all.at[0, core], 0, 0)]
    third[0].start()
    second = [[] for _ in range(runs)]
    for d in range(1, runs):
        first[d][0].wait_recv()
        part = stim_all.at[d, core, mine]
        for v in range(1, parts):
            peer = {"vox": lax.rem(place + v, parts)}
            second[d].append(
                remote(part, part, s2.at[d - 1, v - 1], r2.at[d - 1, v - 1], peer)
            )
            second[d][-1].start()
    for d in range(1, runs):
        first[d][1].wait_recv()
        block = resp_all.at[d - 1, rows]
        third.append(to_core(block, block, 1, d))
        third[-1].start()
    for d in range(1, runs):
        for copy in second[d]:
            copy.wait_recv()
        block = stim_all.at[d, core]
        third.append(to_core(block, block, 0, d))
        third[-1].start()
    for d in range(1, runs):
        first[d][2].wait_recv()
        for copy in first[d]:
            copy.wait_send()
        for copy in second[d]:
            copy.wait_send()
    own.wait()
    for copy in third:
        copy.wait()


def gather(stim, resp, length, runs, parts):
    time, width = stim.shape
    vox = resp.shape[1]
    anyspace = pl.BlockSpec(memory_space=pl.ANY)
    return pl.pallas_call(
        functools.partial(gather_kernel, runs, parts),
        out_shape=(
            jax.ShapeDtypeStruct((runs, 2, time, width), stim.dtype),
            jax.ShapeDtypeStruct((runs - 1, time, vox), resp.dtype),
            jax.ShapeDtypeStruct((runs - 1, 8, 128), jnp.int32),
        ),
        in_specs=[anyspace] * 3,
        out_specs=(anyspace,) * 3,
        scratch_shapes=[pltpu.SemaphoreType.DMA]
        + [pltpu.SemaphoreType.DMA((3, runs - 1))] * 2
        + [pltpu.SemaphoreType.DMA((runs - 1, parts - 1))] * 2
        + [pltpu.SemaphoreType.DMA((2, runs))] * 2,
        compiler_params=pltpu.CompilerParams(collective_id=0, has_side_effects=True),
    )(stim, resp, length)


def invert(block):
    count = B // SUB
    rows = [block[SUB * i : SUB * (i + 1), :] for i in range(count)]
    lane = lax.broadcasted_iota(jnp.int32, (SUB, B), 1)
    sub = lax.broadcasted_iota(jnp.int32, (SUB, B), 0)

    def wide(x):
        return jnp.broadcast_to(x, (SUB, B))

    for s in range(count):
        at = SUB * s
        inside = (lane >= at) & (lane < at + SUB)
        panel = rows[s]
        cols = [wide(panel[:, at + j : at + j + 1]) for j in range(SUB)]
        e = [[wide(cols[j][i : i + 1, :]) for j in range(i + 1)] for i in range(SUB)]
        start = jnp.where(inside, jnp.where(lane == at + sub, 1.0, 0.0), panel)
        r = [wide(start[i : i + 1, :]) for i in range(SUB)]
        scale, low = [], []
        for p in range(SUB):
            q = 1.0 / e[p][p]
            scale.append(q)
            l = {i: e[i][p] * q for i in range(p + 1, SUB)}
            low.append(l)
            for i in range(p + 1, SUB):
                for j in range(p + 1, i + 1):
                    e[i][j] = e[i][j] - l[i] * e[j][p]
            for i in range(p + 1, SUB):
                r[i] = r[i] - l[i] * r[p]
        for p in range(SUB):
            r[p] = r[p] * scale[p]
        for i in range(SUB - 1, 0, -1):
            for p in range(i):
                r[p] = r[p] - low[p][i] * r[i]
        order = [(s + 1 + t) % count for t in range(count - 1)]
        for t in order:
            row = rows[t]
            acc = jnp.where(inside, 0.0, row)
            for p in range(SUB):
                acc = acc - wide(row[:, at + p : at + p + 1]) * r[p]
            rows[t] = acc
        new = r[0]
        for i in range(1, SUB):
            new = jnp.where(sub == i, r[i], new)
        rows[s] = new
    return jnp.concatenate(rows, axis=0)


def solve_kernel(
    lags, grid, pick, stim, resp, lens, own_resp, own_len, w_out, err_out, xs, phi, tgt, m, pinv
):
    others, time, vox = resp.shape
    nlag = lags.shape[0]
    feat = stim.shape[1]
    width = feat * nlag * B
    blocks = width // B
    chunk = others if others <= 4 else 1
    steps = lax.broadcasted_iota(jnp.int32, (time, B), 0)

    def features(run, length, at):
        keep = steps < length
        for f in range(feat):
            xs[pl.ds(8, time), :] = stim[run, f].astype(F32)
            for j in range(nlag):
                moved = xs[pl.ds(8 - lags[j], time), :]
                phi[pl.ds(at, time), pl.ds((f * nlag + j) * B, B)] = jnp.where(
                    keep, moved, 0.0
                ).astype(BF16)

    def products(total, first):
        full = total.shape[0]
        for i in range(0, blocks, 2):
            lhs = total[:, i * B : (i + 2) * B]
            part = lax.dot_general(
                lhs, total[:, i * B :], (((0,), (0,)), ((), ())), preferred_element_type=F32
            )
            if first:
                m[i * B : (i + 2) * B, i * B : width] = part
            else:
                m[i * B : (i + 2) * B, i * B : width] += part
        part = lax.dot_general(
            total, tgt[:full, :], (((0,), (0,)), ((), ())), preferred_element_type=F32
        )
        if first:
            m[:, width:] = part
        else:
            m[:, width:] += part

    xs[pl.ds(0, 8), :] = jnp.zeros((8, B), F32)
    if chunk == others:
        for i in range(others):
            features(i + 1, lens[i, 0:1, :], i * time)
            tgt[pl.ds(i * time, time), :] = resp[i]
        products(phi[...], True)
    else:
        m[...] = jnp.zeros_like(m)

        def one(i, c):
            features(i + 1, lens[i, 0:1, :], 0)
            tgt[...] = resp[i]
            products(phi[...], False)
            return c

        lax.fori_loop(0, others, one, 0)

    count = jnp.sum(lens[:, 0, :], axis=0, keepdims=True).astype(F32)
    ridge = grid[pick[0, lax.axis_index("feat")]] * count
    diag = lax.broadcasted_iota(jnp.int32, (B, B), 0) == lax.broadcasted_iota(
        jnp.int32, (B, B), 1
    )
    shift = jnp.where(diag, ridge, 0.0)

    def step(k, c):
        base = pl.multiple_of(k * B, B)
        pinv[...] = invert(m[pl.ds(base, B), pl.ds(base, B)] + shift)
        for kk in range(blocks):

            @pl.when(k == kk)
            def _():
                lo = (kk + 1) * B
                u = m[kk * B : lo, lo:]
                v = jnp.dot(pinv[...], u, precision=HI, preferred_element_type=F32)
                for i in range(kk + 1, blocks, 2):
                    n = min(2, blocks - i)
                    off = i * B - lo
                    m[i * B : (i + n) * B, i * B :] -= lax.dot_general(
                        u[:, off : off + n * B],
                        v[:, off:],
                        (((0,), (0,)), ((), ())),
                        precision=HI,
                        preferred_element_type=F32,
                    )
                m[kk * B : lo, lo:] = v

        return c

    lax.fori_loop(0, blocks, step, 0)

    for k in range(blocks - 2, -1, -1):
        lo = (k + 1) * B
        m[k * B : lo, width:] -= jnp.dot(
            m[k * B : lo, lo:width], m[lo:, width:], precision=HI, preferred_element_type=F32
        )
    x = m[:, width:]
    for f in range(feat):
        for j in range(nlag):
            w_out[f, pl.ds(j, B, stride=nlag), :] = x[(f * nlag + j) * B : (f * nlag + j + 1) * B]
    top = x.astype(BF16)
    rest = x - top.astype(F32)
    mid = rest.astype(BF16)
    low = (rest - mid.astype(F32)).astype(BF16)
    features(0, own_len[0:1, :], 0)
    made = jnp.dot(
        phi[:time, :], jnp.concatenate([top, mid, low], axis=1), preferred_element_type=F32
    )
    made = made[:, :vox] + (made[:, vox : 2 * vox] + made[:, 2 * vox :])
    target = jnp.where(steps < own_len[0:1, :], own_resp[...].astype(F32), 0.0)
    error = jnp.sum((target - made) ** 2, axis=0, keepdims=True)
    err_out[...] = jnp.broadcast_to(error / own_len[0:1, :].astype(F32), err_out.shape)


def solve(lags, grid, pick, stim, resp, lens, own_resp, own_len):
    others, time, vox = resp.shape
    feat = stim.shape[1]
    width = feat * lags.shape[0] * B
    depth = time * (others if others <= 4 else 1)
    vmem = pl.BlockSpec(memory_space=pltpu.VMEM)
    smem = pl.BlockSpec(memory_space=pltpu.SMEM)
    return pl.pallas_call(
        solve_kernel,
        out_shape=(
            jax.ShapeDtypeStruct((feat, width // feat, vox), F32),
            jax.ShapeDtypeStruct((8, vox), F32),
        ),
        in_specs=[smem] * 3 + [vmem] * 5,
        out_specs=(vmem, vmem),
        scratch_shapes=[
            pltpu.VMEM((time + 8, B), F32),
            pltpu.VMEM((depth, width), BF16),
            pltpu.VMEM((depth, vox), BF16),
            pltpu.VMEM((width, width + vox), F32),
            pltpu.VMEM((B, B), F32),
        ],
        compiler_params=pltpu.CompilerParams(vmem_limit_bytes=56 * 1024 * 1024),
    )(lags, grid, pick, stim, resp, lens, own_resp, own_len)


def swap_kernel(w, err, w_all, err_all, held, got, send, recv, local):
    core = lax.axis_index("feat")
    other = 1 - core
    barrier = pltpu.get_barrier_semaphore()
    pl.semaphore_signal(barrier, inc=1, device_id={"feat": other}, device_id_type=MESH)
    load = pltpu.make_async_copy(w.at[core], held, local.at[0])
    load.start()
    pl.semaphore_wait(barrier, 1)
    copies = [
        pltpu.make_async_remote_copy(
            src_ref=src,
            dst_ref=dst,
            send_sem=send.at[i],
            recv_sem=recv.at[i],
            device_id={"feat": other},
            device_id_type=MESH,
        )
        for i, (src, dst) in enumerate(((w.at[other], w_all.at[core]), (err, got)))
    ]
    for copy in copies:
        copy.start()
    load.wait()
    store = pltpu.make_async_copy(held, w_all.at[core], local.at[1])
    store.start()
    copies[1].wait()
    row = lax.broadcasted_iota(jnp.int32, err_all.shape, 0)
    err_all[...] = jnp.where(row == core, err[0:2, :], got[0:2, :])
    copies[0].wait()
    store.wait()


def swap(w, err):
    anyspace = pl.BlockSpec(memory_space=pl.ANY)
    vmem = pl.BlockSpec(memory_space=pltpu.VMEM)
    return pl.pallas_call(
        swap_kernel,
        out_shape=(
            jax.ShapeDtypeStruct(w.shape, F32),
            jax.ShapeDtypeStruct((2, err.shape[1]), F32),
        ),
        in_specs=[anyspace, vmem],
        out_specs=(anyspace, vmem),
        scratch_shapes=[
            pltpu.VMEM(w.shape[1:], F32),
            pltpu.VMEM(err.shape, F32),
        ]
        + [pltpu.SemaphoreType.DMA((2,))] * 3,
        compiler_params=pltpu.CompilerParams(collective_id=1, has_side_effects=True),
    )(w, err)


def local(stimulus, responses, run_lengths, lag_steps, ridge_grid, ridge_pick):
    runs = lax.axis_size("run")
    length = jnp.broadcast_to(run_lengths.reshape(1, 1), (8, 128))
    stim_all, resp_all, len_all = gather(stimulus[0], responses[0], length, runs, lax.axis_size("vox"))
    w, err = solve(
        lag_steps, ridge_grid, ridge_pick, stim_all, resp_all, len_all, responses[0], length
    )
    w_all, err_all = swap(w, err)
    return (w_all[None], err_all[None])


def solution(mesh):
    return jax.shard_map(
        local,
        mesh=mesh,
        in_specs=(
            P("run", None, "feat"),
            P("run", None, "vox"),
            P("run"),
            P(),
            P(),
            P("run", None),
        ),
        out_specs=(P("run", None, "feat", "vox"), P("run", None, "vox")),
        check_vma=False,
    )
```
